512 devices in a mesh: dp: 32 (over z, x_hi), fsdp: 16 (over x_lo, y, core).
Axes of the slice: x: 4 (x_hi: 2, x_lo: 2; x = x_hi * 2 + x_lo), y: 4, z: 16, core: 2. Of those that a mesh axis runs over, the one named last changes fastest.
Arguments:
- layer_inputs: bfloat16 [65536, 4096], P(('dp', 'fsdp')), may hold values from -6 to 6
- output_grads: bfloat16 [65536, 12288], P(('dp', 'fsdp')), may hold values from -6 to 6
- slot_block_table: int32 [16], replicated, may hold values from 0 to 15, each once
- weight_gradient_pairs: bfloat16 [48, 1024, 1024], P('fsdp', 'dp'), may hold values from -6 to 6
- basis_in: bfloat16 [4, 1024, 1024], P(None, None, 'dp'), may hold values from -0.1875 to 0.1875
- basis_out: bfloat16 [12, 1024, 1024], P(None, 'dp', 'fsdp'), may hold values from -0.1875 to 0.1875
- values_in: float32 [4, 1024], replicated, may hold values from 0.3 to 3
- values_out: float32 [12, 1024], replicated, may hold values from 0.3 to 3
Outputs:
- covariance: float32 [16, 1024, 1024], P('fsdp', 'dp')
- preconditioned: bfloat16 [48, 1024, 1024], P('fsdp', 'dp')
The draws below stay inside these ranges and needn't reach their ends.
Inputs may be any that keep to these rules, and one draw needn't show every extreme that they name: `slot_block_table`: each of the 16 factor blocks stands in exactly one slot.
All inputs are finite; a program needn't handle non-finite values.
Results may differ from the reference program's by a relative error of at most 0.017.
Values may be sent and summed in bfloat16 or wider, within the bound.
No kernel may reach another device: no remote copies, remote signals or barrier semaphores. Data moves between devices by JAX's collectives and lax.ppermute only.
A program may use at most 64 MiB of HBM per device.

```python
import math
import jax
import jax.numpy as jnp
from jax import lax

D = 4096
F = 12288
BLK = 1024
NBA = 4
NBG = 12
FACTOR_BLOCKS = 16
NPAIR = 48
TOKENS = 65536


def levels(key, extent, shards, least, top_value):
    factor_of = 1.0
    for position, blocks in shards:
        heights = jax.random.uniform(jax.random.fold_in(jax.random.fold_in(key, 6), position), (blocks,), jnp.float32, least / len(shards), top_value / len(shards))
        factor_of = factor_of * jnp.repeat(jnp.exp(heights), extent[position] // blocks).reshape((-1,) + (1,) * (len(extent) - 1 - position))
    return factor_of


def normal_values(stream_key, extent, deviation, most, cuts=(), kind=jnp.bfloat16):
    loudness = levels(stream_key, extent, cuts, -0.22, 0.18) if cuts else 1.0
    result = jax.random.normal(stream_key, extent, jnp.float32) * deviation * loudness
    return jnp.minimum(jnp.maximum(result, -most), most).astype(kind)


def setup_inputs(seed: int = 0) -> dict:
    streams_of = jax.random.split(jax.random.key(seed), 9)
    layer_inputs = normal_values(streams_of[0], (TOKENS, D), 1.0, 6.0, ((0, 512),))
    output_grads = normal_values(streams_of[1], (TOKENS, F), 1.0, 6.0, ((0, 512),))
    slot_block_table = jax.random.permutation(streams_of[2], FACTOR_BLOCKS).astype(jnp.int32)
    weight_gradient_pairs = normal_values(streams_of[3], (NPAIR, BLK, BLK), 1.0, 6.0, ((0, 16), (1, 32)))
    basis_in = normal_values(streams_of[4], (NBA, BLK, BLK), BLK ** -0.5, 0.1875, ((2, 32),))
    basis_out = normal_values(streams_of[5], (NBG, BLK, BLK), BLK ** -0.5, 0.1875, ((1, 32), (2, 16)))
    values_in = jnp.clip(jnp.exp(jax.random.uniform(streams_of[6], (NBA, BLK), jnp.float32, math.log(0.3), math.log(3.0))), 0.3, 3.0)
    values_out = jnp.clip(jnp.exp(jax.random.uniform(streams_of[7], (NBG, BLK), jnp.float32, math.log(0.3), math.log(3.0))), 0.3, 3.0)
    return dict(layer_inputs=layer_inputs, output_grads=output_grads, slot_block_table=slot_block_table, weight_gradient_pairs=weight_gradient_pairs, basis_in=basis_in, basis_out=basis_out, values_in=values_in, values_out=values_out)


damping = 0.1


def gram_matrix_block(columns_slab):
    return jnp.dot(columns_slab.T, columns_slab, preferred_element_type=jnp.float32) / TOKENS


def reference(layer_inputs, output_grads, slot_block_table, weight_gradient_pairs, basis_in, basis_out, values_in, values_out):
    factor_blocks = []
    for which in range(NBA):
        factor_blocks.append(gram_matrix_block(layer_inputs[:, which * BLK:(which + 1) * BLK]))
    for which in range(NBG):
        factor_blocks.append(gram_matrix_block(output_grads[:, which * BLK:(which + 1) * BLK]))
    stacked = jnp.stack(factor_blocks)
    covariance = stacked[slot_block_table]

    def one_pair(pair_id):
        left_id = pair_id // NBG
        right_id = pair_id % NBG
        left_eigen_vectors = basis_in[left_id]
        right_basis = basis_out[right_id]
        rotated = jnp.dot(weight_gradient_pairs[pair_id], right_basis, preferred_element_type=jnp.float32).astype(jnp.bfloat16)
        inner_rot = jnp.dot(left_eigen_vectors.T, rotated, preferred_element_type=jnp.float32).astype(jnp.bfloat16)
        denom = values_in[left_id][:, None] * values_out[right_id][None, :] + damping
        scaled = (inner_rot.astype(jnp.float32) / denom).astype(jnp.bfloat16)
        back_rot = jnp.dot(left_eigen_vectors, scaled, preferred_element_type=jnp.float32).astype(jnp.bfloat16)
        return jnp.dot(back_rot, right_basis.T, preferred_element_type=jnp.float32).astype(jnp.bfloat16)

    preconditioned = lax.map(one_pair, jnp.arange(NPAIR, dtype=jnp.int32))
    return covariance, preconditioned
```

```python
import jax
import jax.numpy as jnp
from jax import lax
from jax.experimental import pallas as pl
from jax.experimental.pallas import tpu as pltpu
from jax.sharding import Mesh, PartitionSpec as P

damping = 0.1
block = 1024
axes = ("z", "xh", "xl", "yh", "yl", "c")
sizes = (16, 2, 2, 2, 2, 2)
dp = ("z", "xh")
fsdp = ("xl", "yh", "yl", "c")
plane = ("xh", "xl", "yh", "yl", "c")
row_group = ("xh", "yl", "c")
col_group = ("xl", "yh")
n_dp = 32
n_fsdp = 16
rows = block // n_dp
mib = 1024 * 1024


def cost(flops, nbytes):
    return pl.CostEstimate(flops=flops, bytes_accessed=nbytes, transcendentals=0)


def in_vmem(count):
    return [pl.BlockSpec(memory_space=pltpu.VMEM)] * count


def nt(a, b):
    return lax.dot_general(a, b, (((1,), (1,)), ((), ())), preferred_element_type=jnp.float32)


def tn(a, b):
    return lax.dot_general(a, b, (((0,), (0,)), ((), ())), preferred_element_type=jnp.float32)


def sort_kernel(table, inputs, grads, out, sems):
    count_in = inputs.shape[1] // block
    for slot in range(out.shape[0]):
        b = table[slot]

        @pl.when(b < count_in)
        def _():
            start = pl.multiple_of(b * block, block)
            pltpu.make_async_copy(
                inputs.at[:, pl.ds(start, block)], out.at[slot], sems.at[slot]
            ).start()

        @pl.when(b >= count_in)
        def _():
            start = pl.multiple_of((b - count_in) * block, block)
            pltpu.make_async_copy(
                grads.at[:, pl.ds(start, block)], out.at[slot], sems.at[slot]
            ).start()

    for slot in range(out.shape[0]):
        pltpu.make_async_copy(
            inputs.at[:, pl.ds(0, block)], out.at[slot], sems.at[slot]
        ).wait()


def sort_slots(table, inputs, grads):
    tokens = inputs.shape[0]
    slots = (inputs.shape[1] + grads.shape[1]) // block
    return pl.pallas_call(
        sort_kernel,
        out_shape=jax.ShapeDtypeStruct((slots, tokens, block), inputs.dtype),
        in_specs=[
            pl.BlockSpec(memory_space=pltpu.SMEM),
            pl.BlockSpec(memory_space=pl.ANY),
            pl.BlockSpec(memory_space=pl.ANY),
        ],
        out_specs=pl.BlockSpec(memory_space=pltpu.VMEM),
        scratch_shapes=[pltpu.SemaphoreType.DMA((slots,))],
        compiler_params=pltpu.CompilerParams(vmem_limit_bytes=24 * mib),
        cost_estimate=cost(0, 4 * slots * tokens * block),
    )(table, inputs, grads)


def gram_kernel(x, out, acc):
    step = pl.program_id(0)

    @pl.when(step == 0)
    def _():
        acc[...] = jnp.zeros_like(acc)

    tile = x[...]
    acc[...] += tn(tile, tile)

    @pl.when(step == pl.num_programs(0) - 1)
    def _():
        out[...] = acc[...].astype(out.dtype)


def gram(x):
    tokens = x.shape[0]
    chunk = 512
    return pl.pallas_call(
        gram_kernel,
        grid=(tokens // chunk,),
        out_shape=jax.ShapeDtypeStruct((block, block), jnp.bfloat16),
        in_specs=[pl.BlockSpec((chunk, block), lambda i: (i, 0))],
        out_specs=pl.BlockSpec((block, block), lambda i: (0, 0)),
        scratch_shapes=[pltpu.VMEM((block, block), jnp.float32)],
        compiler_params=pltpu.CompilerParams(vmem_limit_bytes=40 * mib),
        cost_estimate=cost(2 * tokens * block * block, 2 * tokens * block + 2 * block * block),
    )(x)


def rotate_kernel(own, w, right, out):
    half = block // 2
    for p in range(w.shape[1]):
        left = jnp.concatenate([w[own[0] ^ j, p] for j in range(4)], axis=0)
        upper = right[:4, p].reshape(-1, half)
        lower = right[4:, p].reshape(-1, half)
        y = nt(upper, left[:, :half]) + nt(lower, left[:, half:])
        out[:, p] = y.astype(out.dtype).reshape(out.shape[0], rows, -1)


def rotate(own, w, right):
    pairs = w.shape[1]
    return pl.pallas_call(
        rotate_kernel,
        out_shape=jax.ShapeDtypeStruct((8, pairs, rows, 4 * rows), jnp.bfloat16),
        in_specs=[pl.BlockSpec(memory_space=pltpu.SMEM)] + in_vmem(2),
        out_specs=in_vmem(1)[0],
        compiler_params=pltpu.CompilerParams(vmem_limit_bytes=24 * mib),
        cost_estimate=cost(2 * pairs * 256 * 128 * block, 5 * mib // 2),
    )(own, w, right)


def middle_kernel(x, left_t, vals_left, vals_right, out):
    groups, pairs = x.shape[0], x.shape[1]
    width = x.shape[3]
    slab = jnp.concatenate([x[i].reshape(pairs * rows, width) for i in range(groups)], axis=1)
    inner = nt(slab, left_t[...]).astype(jnp.bfloat16)
    denom = vals_right[...] * vals_left[...] + damping
    scaled = (inner.astype(jnp.float32) / denom).astype(jnp.bfloat16)
    back = jnp.dot(scaled, left_t[...], preferred_element_type=jnp.float32).astype(out.dtype)
    for i in range(groups):
        out[i] = back[:, i * width : (i + 1) * width].reshape(pairs, rows, width)


def middle(x, left_t, vals_left, vals_right):
    return pl.pallas_call(
        middle_kernel,
        out_shape=jax.ShapeDtypeStruct(x.shape, x.dtype),
        in_specs=in_vmem(4),
        out_specs=in_vmem(1)[0],
        compiler_params=pltpu.CompilerParams(vmem_limit_bytes=24 * mib),
        cost_estimate=cost(4 * 96 * block * block, 5 * mib // 2),
    )(x, left_t, vals_left, vals_right)


def restore_kernel(x, right, out):
    half = block // 2
    for p in range(x.shape[1]):
        back_t = x[:, p].reshape(-1, x.shape[3])
        upper = right[:4, p].reshape(-1, half)
        lower = right[4:, p].reshape(-1, half)
        out[:, p, :, :half] = tn(back_t, upper).astype(out.dtype).reshape(4, rows, half)
        out[:, p, :, half:] = tn(back_t, lower).astype(out.dtype).reshape(4, rows, half)


def restore(x, right):
    pairs = x.shape[1]
    return pl.pallas_call(
        restore_kernel,
        out_shape=jax.ShapeDtypeStruct((4, pairs, rows, block), x.dtype),
        in_specs=in_vmem(2),
        out_specs=in_vmem(1)[0],
        compiler_params=pltpu.CompilerParams(vmem_limit_bytes=24 * mib),
        cost_estimate=cost(2 * pairs * 256 * 128 * block, 5 * mib // 2),
    )(x, right)


def total(x):
    return jnp.sum(x.astype(jnp.float32), axis=0)


def spread(x, names, count):
    copies = jnp.broadcast_to(x[None], (count,) + x.shape)
    return lax.all_to_all(copies, names, split_axis=0, concat_axis=0, tiled=True)


def body(
    layer_inputs,
    output_grads,
    slot_block_table,
    weight_gradient_pairs,
    basis_in,
    basis_out,
    values_in,
    values_out,
):
    tokens_dev = layer_inputs.shape[0]
    count_out = values_out.shape[0]
    pairs = weight_gradient_pairs.shape[0]
    cols = basis_out.shape[2]
    total_tokens = tokens_dev * n_dp * n_fsdp

    there = [
        (z * 32 + h * 16 + f, f * 32 + h * 16 + z)
        for z in range(16)
        for h in range(2)
        for f in range(16)
    ]
    back_again = [(b, a) for a, b in there]

    position = lax.axis_index(fsdp) * pairs
    left_cols = lax.dynamic_index_in_dim(basis_in, position // count_out, 0, keepdims=False)
    left_rows = jnp.transpose(left_cols.reshape(4, 4, 2, rows, rows), (4, 2, 1, 0, 3))

    w = weight_gradient_pairs.reshape(pairs, rows, 16, 2, rows)
    w = jnp.transpose(w, (0, 1, 3, 2, 4)).reshape(pairs, rows, block)
    moved = lax.ppermute(
        jnp.concatenate([w, left_rows.reshape(1, rows, block)], axis=0), axes, there
    )

    groups = count_out // pairs
    here = lax.axis_index("z")
    wanted = basis_out.reshape(groups, pairs * rows * cols // 128, 128)
    pieces = []
    for m in range(4):
        piece = lax.dynamic_index_in_dim(wanted, (here ^ m) % groups, 0, keepdims=False)
        pieces.append(lax.ppermute(piece, "z", [(i, i ^ m) for i in range(16)]) if m else piece)
    pieces = jnp.stack(pieces)
    far = [lax.ppermute(pieces, "z", [(i, i ^ m) for i in range(16)]) for m in (4, 8, 12)]
    came = jnp.concatenate([pieces] + far)
    moved, came = lax.optimization_barrier((moved, came))
    w = moved[:pairs]
    left_t = lax.all_gather(moved[pairs], plane, axis=0, tiled=True)
    others = [
        lax.ppermute(w, col_group, [(j, j ^ m) for j in range(4)]) for m in range(1, 4)
    ]
    w = jnp.stack([w] + others)
    came = jnp.take(came, here ^ jnp.arange(16), axis=0, mode="clip")
    came = jnp.transpose(came.reshape(16, pairs, rows, cols), (1, 3, 0, 2))
    came = came.reshape(pairs, cols, block // 2)

    sorted_slots = sort_slots(slot_block_table, layer_inputs, output_grads)
    gathered = lax.all_to_all(sorted_slots, fsdp, split_axis=0, concat_axis=0, tiled=True)
    gathered, w, came = lax.optimization_barrier((gathered, w, came))
    right = spread(came, row_group, 8)
    partial = gram(gathered.reshape(-1, block))
    mine = lax.psum_scatter(partial, "z", scatter_dimension=0, tiled=True)
    mine = mine.reshape(2, rows, block)
    own = lax.axis_index("xh")
    sent = lax.dynamic_index_in_dim(mine, 1 - own, 0, keepdims=True)
    kept = lax.dynamic_index_in_dim(mine, own, 0, keepdims=True)
    came_cov = lax.ppermute(sent, "xh", [(0, 1), (1, 0)])
    covariance = (kept.astype(jnp.float32) + came_cov.astype(jnp.float32)) / total_tokens

    pair = lax.axis_index("z") * pairs
    start = lax.axis_index(col_group) * 256 + lax.axis_index(row_group) * rows
    right_vals = lax.dynamic_slice(values_out, (pair % count_out, start), (pairs, rows))
    left_vals = lax.dynamic_index_in_dim(values_in, pair // count_out, 0, keepdims=False)
    left_vals = jnp.transpose(left_vals.reshape(16, 2, rows), (1, 0, 2))

    rotated = rotate(lax.axis_index(col_group).reshape(1), w, right)
    slab = lax.all_to_all(rotated, row_group, split_axis=0, concat_axis=0, tiled=True)
    back_rot = middle(
        slab, left_t, left_vals.reshape(1, block), right_vals.reshape(pairs * rows, 1)
    )
    again = lax.all_to_all(back_rot, row_group, split_axis=0, concat_axis=0, tiled=True)
    parts = restore(again, right)
    parts = lax.all_to_all(parts, col_group, split_axis=0, concat_axis=0, tiled=True)
    result = total(parts).astype(jnp.bfloat16).reshape(pairs, rows, 2, 16, rows)
    result = jnp.transpose(result, (0, 1, 3, 2, 4)).reshape(pairs, rows, block)
    preconditioned = lax.ppermute(result, axes, back_again)
    return covariance, preconditioned


def solution(mesh):
    fine = Mesh(mesh.devices.reshape(sizes), axes)
    everywhere = P(axes, None)
    placed = (
        everywhere,
        everywhere,
        P(),
        P(fsdp, dp, None),
        P(None, None, dp),
        P(None, dp, fsdp),
        P(),
        P(),
    )
    return jax.shard_map(
        body,
        mesh=fine,
        in_specs=placed,
        out_specs=(P(fsdp, dp, None), P(fsdp, dp, None)),
        check_vma=False,
    )
```

```python
import jax
import jax.numpy as jnp
from jax import lax
from jax.experimental import pallas as pl
from jax.experimental.pallas import tpu as pltpu
from jax.sharding import Mesh, PartitionSpec as P

damping = 0.1
block = 1024
axes = ("z", "xh", "xl", "yh", "yl", "c")
sizes = (16, 2, 2, 2, 2, 2)
dp = ("z", "xh")
fsdp = ("xl", "yh", "yl", "c")
plane = ("xh", "xl", "yh", "yl", "c")
row_group = ("xh", "yl", "c")
col_group = ("xl", "yh")
n_dp = 32
n_fsdp = 16
rows = block // n_dp
mib = 1024 * 1024


def cost(flops, nbytes):
    return pl.CostEstimate(flops=flops, bytes_accessed=nbytes, transcendentals=0)


def in_vmem(count):
    return [pl.BlockSpec(memory_space=pltpu.VMEM)] * count


def nt(a, b):
    return lax.dot_general(a, b, (((1,), (1,)), ((), ())), preferred_element_type=jnp.float32)


def tn(a, b):
    return lax.dot_general(a, b, (((0,), (0,)), ((), ())), preferred_element_type=jnp.float32)


def sort_kernel(table, inputs, grads, out, sems):
    count_in = inputs.shape[1] // block
    for slot in range(out.shape[0]):
        b = table[slot]

        @pl.when(b < count_in)
        def _():
            start = pl.multiple_of(b * block, block)
            pltpu.make_async_copy(
                inputs.at[:, pl.ds(start, block)], out.at[slot], sems.at[slot]
            ).start()

        @pl.when(b >= count_in)
        def _():
            start = pl.multiple_of((b - count_in) * block, block)
            pltpu.make_async_copy(
                grads.at[:, pl.ds(start, block)], out.at[slot], sems.at[slot]
            ).start()

    for slot in range(out.shape[0]):
        pltpu.make_async_copy(
            inputs.at[:, pl.ds(0, block)], out.at[slot], sems.at[slot]
        ).wait()


def sort_slots(table, inputs, grads):
    tokens = inputs.shape[0]
    slots = (inputs.shape[1] + grads.shape[1]) // block
    return pl.pallas_call(
        sort_kernel,
        out_shape=jax.ShapeDtypeStruct((slots, tokens, block), inputs.dtype),
        in_specs=[
            pl.BlockSpec(memory_space=pltpu.SMEM),
            pl.BlockSpec(memory_space=pl.ANY),
            pl.BlockSpec(memory_space=pl.ANY),
        ],
        out_specs=pl.BlockSpec(memory_space=pltpu.VMEM),
        scratch_shapes=[pltpu.SemaphoreType.DMA((slots,))],
        compiler_params=pltpu.CompilerParams(vmem_limit_bytes=24 * mib),
        cost_estimate=cost(0, 4 * slots * tokens * block),
    )(table, inputs, grads)


def gram_kernel(x, out, acc):
    step = pl.program_id(0)

    @pl.when(step == 0)
    def _():
        acc[...] = jnp.zeros_like(acc)

    tile = x[...]
    acc[...] += tn(tile, tile)

    @pl.when(step == pl.num_programs(0) - 1)
    def _():
        out[...] = acc[...].astype(out.dtype)


def gram(x):
    tokens = x.shape[0]
    chunk = 512
    return pl.pallas_call(
        gram_kernel,
        grid=(tokens // chunk,),
        out_shape=jax.ShapeDtypeStruct((block, block), jnp.bfloat16),
        in_specs=[pl.BlockSpec((chunk, block), lambda i: (i, 0))],
        out_specs=pl.BlockSpec((block, block), lambda i: (0, 0)),
        scratch_shapes=[pltpu.VMEM((block, block), jnp.float32)],
        compiler_params=pltpu.CompilerParams(vmem_limit_bytes=40 * mib),
        cost_estimate=cost(2 * tokens * block * block, 2 * tokens * block + 2 * block * block),
    )(x)


def rotate_kernel(own, w, right, out):
    half = block // 2
    for p in range(w.shape[1]):
        left = jnp.concatenate([w[own[0] ^ j, p] for j in range(4)], axis=0)
        upper = right[:4, p].reshape(-1, half)
        lower = right[4:, p].reshape(-1, half)
        y = nt(upper, left[:, :half]) + nt(lower, left[:, half:])
        out[:, p] = y.astype(out.dtype).reshape(out.shape[0], rows, -1)


def rotate(own, w, right):
    pairs = w.shape[1]
    return pl.pallas_call(
        rotate_kernel,
        out_shape=jax.ShapeDtypeStruct((8, pairs, rows, 4 * rows), jnp.bfloat16),
        in_specs=[pl.BlockSpec(memory_space=pltpu.SMEM)] + in_vmem(2),
        out_specs=in_vmem(1)[0],
        compiler_params=pltpu.CompilerParams(vmem_limit_bytes=24 * mib),
        cost_estimate=cost(2 * pairs * 256 * 128 * block, 5 * mib // 2),
    )(own, w, right)


def middle_kernel(x, left_t, vals_left, vals_right, out):
    groups, pairs = x.shape[0], x.shape[1]
    width = x.shape[3]
    slab = jnp.concatenate([x[i].reshape(pairs * rows, width) for i in range(groups)], axis=1)
    inner = nt(slab, left_t[...]).astype(jnp.bfloat16)
    denom = vals_right[...] * vals_left[...] + damping
    scaled = (inner.astype(jnp.float32) / denom).astype(jnp.bfloat16)
    back = jnp.dot(scaled, left_t[...], preferred_element_type=jnp.float32).astype(out.dtype)
    for i in range(groups):
        out[i] = back[:, i * width : (i + 1) * width].reshape(pairs, rows, width)


def middle(x, left_t, vals_left, vals_right):
    return pl.pallas_call(
        middle_kernel,
        out_shape=jax.ShapeDtypeStruct(x.shape, x.dtype),
        in_specs=in_vmem(4),
        out_specs=in_vmem(1)[0],
        compiler_params=pltpu.CompilerParams(vmem_limit_bytes=24 * mib),
        cost_estimate=cost(4 * 96 * block * block, 5 * mib // 2),
    )(x, left_t, vals_left, vals_right)


def restore_kernel(x, right, out):
    half = block // 2
    for p in range(x.shape[1]):
        back_t = x[:, p].reshape(-1, x.shape[3])
        upper = right[:4, p].reshape(-1, half)
        lower = right[4:, p].reshape(-1, half)
        out[:, p, :, :half] = tn(back_t, upper).astype(out.dtype).reshape(4, rows, half)
        out[:, p, :, half:] = tn(back_t, lower).astype(out.dtype).reshape(4, rows, half)


def restore(x, right):
    pairs = x.shape[1]
    return pl.pallas_call(
        restore_kernel,
        out_shape=jax.ShapeDtypeStruct((4, pairs, rows, block), x.dtype),
        in_specs=in_vmem(2),
        out_specs=in_vmem(1)[0],
        compiler_params=pltpu.CompilerParams(vmem_limit_bytes=24 * mib),
        cost_estimate=cost(2 * pairs * 256 * 128 * block, 5 * mib // 2),
    )(x, right)


def total(x):
    return jnp.sum(x.astype(jnp.float32), axis=0)


def spread(x, names, count):
    copies = jnp.broadcast_to(x[None], (count,) + x.shape)
    return lax.all_to_all(copies, names, split_axis=0, concat_axis=0, tiled=True)


def body(
    layer_inputs,
    output_grads,
    slot_block_table,
    weight_gradient_pairs,
    basis_in,
    basis_out,
    values_in,
    values_out,
):
    tokens_dev = layer_inputs.shape[0]
    count_out = values_out.shape[0]
    pairs = weight_gradient_pairs.shape[0]
    cols = basis_out.shape[2]
    total_tokens = tokens_dev * n_dp * n_fsdp

    there = [
        (z * 32 + h * 16 + f, f * 32 + h * 16 + (z ^ f))
        for z in range(16)
        for h in range(2)
        for f in range(16)
    ]
    back_again = [(b, a) for a, b in there]

    order = jnp.arange(16)
    target = lax.axis_index(fsdp)
    left_cols = lax.dynamic_index_in_dim(
        basis_in, target * pairs // count_out, 0, keepdims=False
    )
    left_cols = jnp.take(left_cols.reshape(16, 2 * rows, rows), target ^ order, axis=0, mode="clip")
    left_rows = jnp.transpose(left_cols.reshape(4, 4, 2, rows, rows), (4, 2, 1, 0, 3))

    w = weight_gradient_pairs.reshape(pairs, rows, 16, 2, rows)
    w = jnp.transpose(w, (0, 1, 3, 2, 4)).reshape(pairs, rows, block)
    moved = lax.ppermute(
        jnp.concatenate([w, left_rows.reshape(1, rows, block)], axis=0), axes, there
    )

    groups = count_out // pairs
    here = lax.axis_index("z")
    wanted = basis_out.reshape(groups, pairs * rows * cols // 128, 128)
    pieces = []
    for m in range(4):
        piece = lax.dynamic_index_in_dim(wanted, (here ^ m) % groups, 0, keepdims=False)
        pieces.append(lax.ppermute(piece, "z", [(i, i ^ m) for i in range(16)]) if m else piece)
    pieces = jnp.stack(pieces)
    far = [lax.ppermute(pieces, "z", [(i, i ^ m) for i in range(16)]) for m in (4, 8, 12)]
    came = jnp.concatenate([pieces] + far)
    moved, came = lax.optimization_barrier((moved, came))
    w = moved[:pairs]
    left_t = lax.all_gather(moved[pairs], plane, axis=0, tiled=True)
    came = jnp.take(came, here ^ order, axis=0, mode="clip")
    came = jnp.transpose(came.reshape(16, pairs, rows, cols), (1, 3, 0, 2))
    came = came.reshape(pairs, cols, block // 2)

    sorted_slots = sort_slots(slot_block_table, layer_inputs, output_grads)
    gathered = lax.all_to_all(sorted_slots, fsdp, split_axis=0, concat_axis=0, tiled=True)
    gathered, w, came = lax.optimization_barrier((gathered, w, came))
    right = spread(came, row_group, 8)
    others = [
        lax.ppermute(w, col_group, [(j, j ^ m) for j in range(4)]) for m in range(1, 4)
    ]
    w = jnp.stack([w] + others)
    partial = gram(gathered.reshape(-1, block))
    mine = lax.psum_scatter(partial, "z", scatter_dimension=0, tiled=True)
    mine = mine.reshape(2, rows, block)
    own = lax.axis_index("xh")
    sent = lax.dynamic_index_in_dim(mine, 1 - own, 0, keepdims=True)
    kept = lax.dynamic_index_in_dim(mine, own, 0, keepdims=True)
    came_cov = lax.ppermute(sent, "xh", [(0, 1), (1, 0)])
    covariance = (kept.astype(jnp.float32) + came_cov.astype(jnp.float32)) / total_tokens

    pair = lax.axis_index("z") * pairs
    start = lax.axis_index(col_group) * 256 + lax.axis_index(row_group) * rows
    right_vals = lax.dynamic_slice(values_out, (pair % count_out, start), (pairs, rows))
    left_vals = lax.dynamic_index_in_dim(values_in, pair // count_out, 0, keepdims=False)
    left_vals = jnp.take(left_vals.reshape(16, 2, rows), here ^ order, axis=0, mode="clip")
    left_vals = jnp.transpose(left_vals, (1, 0, 2))

    rotated = rotate(lax.axis_index(col_group).reshape(1), w, right)
    slab = lax.all_to_all(rotated, row_group, split_axis=0, concat_axis=0, tiled=True)
    back_rot = middle(
        slab, left_t, left_vals.reshape(1, block), right_vals.reshape(pairs * rows, 1)
    )
    again = lax.all_to_all(back_rot, row_group, split_axis=0, concat_axis=0, tiled=True)
    parts = restore(again, right)
    parts = lax.all_to_all(parts, col_group, split_axis=0, concat_axis=0, tiled=True)
    result = total(parts).astype(jnp.bfloat16)
    result = lax.ppermute(result.reshape(pairs, rows, block), axes, back_again)
    result = jnp.transpose(result.reshape(pairs, rows, 2, 16, rows), (0, 1, 3, 2, 4))
    return covariance, result.reshape(pairs, rows, block)


def solution(mesh):
    fine = Mesh(mesh.devices.reshape(sizes), axes)
    everywhere = P(axes, None)
    placed = (
        everywhere,
        everywhere,
        P(),
        P(fsdp, dp, None),
        P(None, None, dp),
        P(None, dp, fsdp),
        P(),
        P(),
    )
    return jax.shard_map(
        body,
        mesh=fine,
        in_specs=placed,
        out_specs=(P(fsdp, dp, None), P(fsdp, dp, None)),
        check_vma=False,
    )
```

```python
import jax
import jax.numpy as jnp
from jax import lax
from jax.experimental import pallas as pl
from jax.experimental.pallas import tpu as pltpu
from jax.sharding import Mesh, PartitionSpec as P

damping = 0.1
block = 1024
axes = ("z", "xh", "xl", "yh", "yl", "c")
sizes = (16, 2, 2, 2, 2, 2)
dp = ("z", "xh")
fsdp = ("xl", "yh", "yl", "c")
plane = ("xh", "xl", "yh", "yl", "c")
row_group = ("xh", "yl", "c")
col_group = ("xl", "yh")
n_dp = 32
n_fsdp = 16
rows = block // n_dp
mib = 1024 * 1024


def cost(flops, nbytes):
    return pl.CostEstimate(flops=flops, bytes_accessed=nbytes, transcendentals=0)


def in_vmem(count):
    return [pl.BlockSpec(memory_space=pltpu.VMEM)] * count


def nt(a, b):
    return lax.dot_general(a, b, (((1,), (1,)), ((), ())), preferred_element_type=jnp.float32)


def tn(a, b):
    return lax.dot_general(a, b, (((0,), (0,)), ((), ())), preferred_element_type=jnp.float32)


def sort_kernel(table, inputs, grads, out, sems):
    count_in = inputs.shape[1] // block
    for slot in range(out.shape[0]):
        b = table[slot]

        @pl.when(b < count_in)
        def _():
            start = pl.multiple_of(b * block, block)
            pltpu.make_async_copy(
                inputs.at[:, pl.ds(start, block)], out.at[slot], sems.at[slot]
            ).start()

        @pl.when(b >= count_in)
        def _():
            start = pl.multiple_of((b - count_in) * block, block)
            pltpu.make_async_copy(
                grads.at[:, pl.ds(start, block)], out.at[slot], sems.at[slot]
            ).start()

    for slot in range(out.shape[0]):
        pltpu.make_async_copy(
            inputs.at[:, pl.ds(0, block)], out.at[slot], sems.at[slot]
        ).wait()


def sort_slots(table, inputs, grads):
    tokens = inputs.shape[0]
    slots = (inputs.shape[1] + grads.shape[1]) // block
    return pl.pallas_call(
        sort_kernel,
        out_shape=jax.ShapeDtypeStruct((slots, tokens, block), inputs.dtype),
        in_specs=[
            pl.BlockSpec(memory_space=pltpu.SMEM),
            pl.BlockSpec(memory_space=pl.ANY),
            pl.BlockSpec(memory_space=pl.ANY),
        ],
        out_specs=pl.BlockSpec(memory_space=pltpu.VMEM),
        scratch_shapes=[pltpu.SemaphoreType.DMA((slots,))],
        compiler_params=pltpu.CompilerParams(vmem_limit_bytes=24 * mib),
        cost_estimate=cost(0, 4 * slots * tokens * block),
    )(table, inputs, grads)


def gram_kernel(x, out, acc):
    step = pl.program_id(0)

    @pl.when(step == 0)
    def _():
        acc[...] = jnp.zeros_like(acc)

    tile = x[...]
    acc[...] += tn(tile, tile)

    @pl.when(step == pl.num_programs(0) - 1)
    def _():
        out[...] = acc[...].astype(out.dtype)


def gram(x):
    tokens = x.shape[0]
    chunk = 512
    return pl.pallas_call(
        gram_kernel,
        grid=(tokens // chunk,),
        out_shape=jax.ShapeDtypeStruct((block, block), jnp.bfloat16),
        in_specs=[pl.BlockSpec((chunk, block), lambda i: (i, 0))],
        out_specs=pl.BlockSpec((block, block), lambda i: (0, 0)),
        scratch_shapes=[pltpu.VMEM((block, block), jnp.float32)],
        compiler_params=pltpu.CompilerParams(vmem_limit_bytes=40 * mib),
        cost_estimate=cost(2 * tokens * block * block, 2 * tokens * block + 2 * block * block),
    )(x)


def rotate_kernel(own, w, right, out):
    half = block // 2
    for p in range(w.shape[1]):
        left = jnp.concatenate([w[own[0] ^ j, p] for j in range(4)], axis=0)
        upper = right[:4, p].reshape(-1, half)
        lower = right[4:, p].reshape(-1, half)
        y = nt(upper, left[:, :half]) + nt(lower, left[:, half:])
        out[:, p] = y.astype(out.dtype).reshape(out.shape[0], rows, -1)


def rotate(own, w, right):
    pairs = w.shape[1]
    return pl.pallas_call(
        rotate_kernel,
        out_shape=jax.ShapeDtypeStruct((8, pairs, rows, 4 * rows), jnp.bfloat16),
        in_specs=[pl.BlockSpec(memory_space=pltpu.SMEM)] + in_vmem(2),
        out_specs=in_vmem(1)[0],
        compiler_params=pltpu.CompilerParams(vmem_limit_bytes=24 * mib),
        cost_estimate=cost(2 * pairs * 256 * 128 * block, 5 * mib // 2),
    )(own, w, right)


def middle_kernel(x, left_t, vals_left, vals_right, out):
    groups, pairs = x.shape[0], x.shape[1]
    width = x.shape[3]
    slab = jnp.concatenate([x[i].reshape(pairs * rows, width) for i in range(groups)], axis=1)
    inner = nt(slab, left_t[...]).astype(jnp.bfloat16)
    denom = vals_right[...] * vals_left[...] + damping
    scaled = (inner.astype(jnp.float32) / denom).astype(jnp.bfloat16)
    back = jnp.dot(scaled, left_t[...], preferred_element_type=jnp.float32).astype(out.dtype)
    for i in range(groups):
        out[i] = back[:, i * width : (i + 1) * width].reshape(pairs, rows, width)


def middle(x, left_t, vals_left, vals_right):
    return pl.pallas_call(
        middle_kernel,
        out_shape=jax.ShapeDtypeStruct(x.shape, x.dtype),
        in_specs=in_vmem(4),
        out_specs=in_vmem(1)[0],
        compiler_params=pltpu.CompilerParams(vmem_limit_bytes=24 * mib),
        cost_estimate=cost(4 * 96 * block * block, 5 * mib // 2),
    )(x, left_t, vals_left, vals_right)


def restore_kernel(x, right, out):
    half = block // 2
    for p in range(x.shape[1]):
        back_t = x[:, p].reshape(-1, x.shape[3])
        upper = right[:4, p].reshape(-1, half)
        lower = right[4:, p].reshape(-1, half)
        out[:, p, :, :half] = tn(back_t, upper).astype(out.dtype).reshape(4, rows, half)
        out[:, p, :, half:] = tn(back_t, lower).astype(out.dtype).reshape(4, rows, half)


def restore(x, right):
    pairs = x.shape[1]
    return pl.pallas_call(
        restore_kernel,
        out_shape=jax.ShapeDtypeStruct((4, pairs, rows, block), x.dtype),
        in_specs=in_vmem(2),
        out_specs=in_vmem(1)[0],
        compiler_params=pltpu.CompilerParams(vmem_limit_bytes=24 * mib),
        cost_estimate=cost(2 * pairs * 256 * 128 * block, 5 * mib // 2),
    )(x, right)


def total(x):
    return jnp.sum(x.astype(jnp.float32), axis=0)


def spread(x, names, count):
    copies = jnp.broadcast_to(x[None], (count,) + x.shape)
    return lax.all_to_all(copies, names, split_axis=0, concat_axis=0, tiled=True)


def body(
    layer_inputs,
    output_grads,
    slot_block_table,
    weight_gradient_pairs,
    basis_in,
    basis_out,
    values_in,
    values_out,
):
    tokens_dev = layer_inputs.shape[0]
    count_out = values_out.shape[0]
    pairs = weight_gradient_pairs.shape[0]
    cols = basis_out.shape[2]
    total_tokens = tokens_dev * n_dp * n_fsdp

    there = [
        (z * 32 + h * 16 + f, f * 32 + h * 16 + (z ^ f))
        for z in range(16)
        for h in range(2)
        for f in range(16)
    ]
    back_again = [(b, a) for a, b in there]

    order = jnp.arange(16)
    target = lax.axis_index(fsdp)
    left_cols = lax.dynamic_index_in_dim(
        basis_in, target * pairs // count_out, 0, keepdims=False
    )
    left_cols = jnp.take(left_cols.reshape(16, 2 * rows, rows), target ^ order, axis=0, mode="clip")
    left_rows = jnp.transpose(left_cols.reshape(4, 4, 2, rows, rows), (4, 2, 1, 0, 3))

    w = weight_gradient_pairs.reshape(pairs, rows, 16, 2, rows)
    w = jnp.transpose(w, (0, 1, 3, 2, 4)).reshape(pairs, rows, block)
    moved = lax.ppermute(
        jnp.concatenate([w, left_rows.reshape(1, rows, block)], axis=0), axes, there
    )

    groups = count_out // pairs
    here = lax.axis_index("z")
    wanted = basis_out.reshape(groups, pairs * rows * cols // 128, 128)
    pieces = []
    for m in range(4):
        piece = lax.dynamic_index_in_dim(wanted, (here ^ m) % groups, 0, keepdims=False)
        pieces.append(lax.ppermute(piece, "z", [(i, i ^ m) for i in range(16)]) if m else piece)
    pieces = jnp.stack(pieces)
    moved, _ = lax.optimization_barrier((moved, pieces))
    w = moved[:pairs]
    left_t = lax.all_gather(moved[pairs], plane, axis=0, tiled=True)
    far = [lax.ppermute(pieces, "z", [(i, i ^ m) for i in range(16)]) for m in (4, 8, 12)]
    came = jnp.concatenate([pieces] + far)
    came = jnp.take(came, here ^ order, axis=0, mode="clip")
    came = jnp.transpose(came.reshape(16, pairs, rows, cols), (1, 3, 0, 2))
    came = came.reshape(pairs, cols, block // 2)

    sorted_slots = sort_slots(slot_block_table, layer_inputs, output_grads)
    gathered = lax.all_to_all(sorted_slots, fsdp, split_axis=0, concat_axis=0, tiled=True)
    gathered, w, came = lax.optimization_barrier((gathered, w, came))
    right = spread(came, row_group, 8)
    others = [
        lax.ppermute(w, col_group, [(j, j ^ m) for j in range(4)]) for m in range(1, 4)
    ]
    w = jnp.stack([w] + others)
    partial = gram(gathered.reshape(-1, block))
    mine = lax.psum_scatter(partial, "z", scatter_dimension=0, tiled=True)
    mine = mine.reshape(2, rows, block)
    own = lax.axis_index("xh")
    sent = lax.dynamic_index_in_dim(mine, 1 - own, 0, keepdims=True)
    kept = lax.dynamic_index_in_dim(mine, own, 0, keepdims=True)
    came_cov = lax.ppermute(sent, "xh", [(0, 1), (1, 0)])
    covariance = (kept.astype(jnp.float32) + came_cov.astype(jnp.float32)) / total_tokens

    pair = lax.axis_index("z") * pairs
    start = lax.axis_index(col_group) * 256 + lax.axis_index(row_group) * rows
    right_vals = lax.dynamic_slice(values_out, (pair % count_out, start), (pairs, rows))
    left_vals = lax.dynamic_index_in_dim(values_in, pair // count_out, 0, keepdims=False)
    left_vals = jnp.take(left_vals.reshape(16, 2, rows), here ^ order, axis=0, mode="clip")
    left_vals = jnp.transpose(left_vals, (1, 0, 2))

    rotated = rotate(lax.axis_index(col_group).reshape(1), w, right)
    slab = lax.all_to_all(rotated, row_group, split_axis=0, concat_axis=0, tiled=True)
    back_rot = middle(
        slab, left_t, left_vals.reshape(1, block), right_vals.reshape(pairs * rows, 1)
    )
    again = lax.all_to_all(back_rot, row_group, split_axis=0, concat_axis=0, tiled=True)
    parts = restore(again, right)
    parts = lax.all_to_all(parts, col_group, split_axis=0, concat_axis=0, tiled=True)
    result = total(parts).astype(jnp.bfloat16)
    result = lax.ppermute(result.reshape(pairs, rows, block), axes, back_again)
    result = jnp.transpose(result.reshape(pairs, rows, 2, 16, rows), (0, 1, 3, 2, 4))
    return covariance, result.reshape(pairs, rows, block)


def solution(mesh):
    fine = Mesh(mesh.devices.reshape(sizes), axes)
    everywhere = P(axes, None)
    placed = (
        everywhere,
        everywhere,
        P(),
        P(fsdp, dp, None),
        P(None, None, dp),
        P(None, dp, fsdp),
        P(),
        P(),
    )
    return jax.shard_map(
        body,
        mesh=fine,
        in_specs=placed,
        out_specs=(P(fsdp, dp, None), P(fsdp, dp, None)),
        check_vma=False,
    )
```
